256 devices in a mesh: region: 8 (over x_hi, y), dev: 32 (over z, x_lo, core).
Axes of the slice: x: 4 (x_hi: 2, x_lo: 2; x = x_hi * 2 + x_lo), y: 4, z: 8, core: 2. Of those that a mesh axis runs over, the one named last changes fastest.
Arguments:
- acts: bfloat16 [8, 2048, 2048], P('region', 'dev'), may hold values from -6 to 6
- cotan: bfloat16 [8, 2048, 2048], P('region', 'dev'), may hold values from -6 to 6
- w_up: bfloat16 [8, 2048, 4096], P('region', None, 'dev'), may hold values from -6 to 6
- w_down: bfloat16 [8, 4096, 2048], P('region', 'dev'), may hold values from -6 to 6
- drift_up: bfloat16 [8, 2048, 4096], P('region', None, 'dev'), may hold values from -4 to 4
- drift_down: bfloat16 [8, 4096, 2048], P('region', 'dev'), may hold values from -4 to 4
- path: int32 [8], replicated, may hold values from 0 to 15
- slot_of: int32 [16], replicated, may hold values from 0 to 15, each once
- global_up: bfloat16 [16, 2048, 4096], P('region', None, 'dev'), may hold values from -6 to 6
- global_down: bfloat16 [16, 4096, 2048], P('region', 'dev'), may hold values from -6 to 6
- mom_up: float32 [16, 2048, 4096], P('region', None, 'dev'), may hold values from -4 to 4
- mom_down: float32 [16, 4096, 2048], P('region', 'dev'), may hold values from -4 to 4
Outputs:
- new_up: bfloat16 [16, 2048, 4096], P('region', None, 'dev')
- new_down: bfloat16 [16, 4096, 2048], P('region', 'dev')
- region_up: bfloat16 [8, 2048, 4096], P('region', None, 'dev')
- region_down: bfloat16 [8, 4096, 2048], P('region', 'dev')
The draws below stay inside these ranges and needn't reach their ends.
Inputs may be any that keep to these rules, and one draw needn't show every extreme that they name: `slot_of`: each module's slot once; slot s lies in region s // 2.
All inputs are finite; a program needn't handle non-finite values.
Results may differ from the reference program's by a relative error of at most 0.0035.
Values may be sent and summed in bfloat16 or wider, within the bound.
No kernel may reach another device: no remote copies, remote signals or barrier semaphores. Data moves between devices by JAX's collectives and lax.ppermute only.
A program may use at most 128 MiB of HBM per device.

```python
import math
import jax
import jax.numpy as jnp
import numpy as np
from jax import lax

D = 2048
FF = 4096
MODULES = 16
TOKENS_R = 2048
N_REGION = 8


def touch_ends(drawn, key, smallest, top_value):
    longest = drawn.shape.index(max(drawn.shape))
    spots = []
    for shift in (0, 1):
        where = [jax.random.randint(jax.random.fold_in(key, axis), (), 0, length) for axis, length in enumerate(drawn.shape)]
        where[longest] = (where[longest] + shift) % drawn.shape[longest]
        spots.append(tuple(where))
    return drawn.at[spots[0]].set(smallest).at[spots[1]].set(top_value)


def steps_of(key, dims, cuts, least, high):
    def one(axis_at, parts):
        draws = jax.random.uniform(jax.random.fold_in(jax.random.fold_in(key, 6), axis_at), (parts,), jnp.float32, least / len(cuts), high / len(cuts))
        return jnp.repeat(jnp.exp(draws), dims[axis_at] // parts).reshape((-1,) + (1,) * (len(dims) - axis_at - 1))

    loudness = one(*cuts[0])
    for cut in cuts[1:]:
        loudness = loudness * one(*cut)
    return loudness


def cumulative_ranks(amount, slope):
    weights = [(1 << 20) // math.isqrt(grade ** slope) + 1 for grade in range(1, amount + 1)]
    spread = 1 + sum(weights) // (1 << 30)
    return np.cumsum(np.array([max(1, weight // spread) for weight in weights]))


def skewed_ids(own_key, extent, count, lean):
    grid = cumulative_ranks(count, lean)
    ticket = jax.random.randint(jax.random.fold_in(own_key, 1), extent, 0, int(grid[count - 1]))
    standing = jnp.searchsorted(jnp.asarray(grid, jnp.int32), ticket, side="right")
    return jax.random.permutation(jax.random.fold_in(own_key, 2), count)[standing].astype(jnp.int32)


def centred(stream_key, extent, scale, reach, pieces=(), held_as=jnp.bfloat16):
    factor_of = steps_of(stream_key, extent, pieces, -0.22, 0.18) if pieces else 1.0
    result = jax.random.normal(stream_key, extent, jnp.float32) * scale * factor_of
    return jnp.minimum(jnp.maximum(result, -reach), reach).astype(held_as)


def setup_inputs(seed: int = 0) -> dict:
    keys = jax.random.split(jax.random.key(seed), 13)
    acts = centred(keys[0], (N_REGION, TOKENS_R, D), 1.0, 6.0, ((0, 8), (1, 32)))
    cotan = centred(keys[1], (N_REGION, TOKENS_R, D), 1.0, 6.0, ((0, 8), (1, 32)))
    w_up = centred(keys[2], (N_REGION, D, FF), 1.0, 6.0, ((0, 8), (2, 32)))
    w_down = centred(keys[3], (N_REGION, FF, D), 1.0, 6.0, ((0, 8), (1, 32)))
    drift_up = centred(keys[4], (N_REGION, D, FF), 0.5, 4.0, ((0, 8), (2, 32)))
    drift_down = centred(keys[5], (N_REGION, FF, D), 0.5, 4.0, ((0, 8), (1, 32)))
    path = touch_ends(skewed_ids(keys[6], (N_REGION,), MODULES, 2), jax.random.fold_in(keys[6], 3), 0, MODULES - 1).astype(jnp.int32)
    slot_of = jax.random.permutation(keys[7], MODULES).astype(jnp.int32)
    global_up = centred(keys[8], (MODULES, D, FF), 1.0, 6.0, ((0, 8), (2, 32)))
    global_down = centred(keys[9], (MODULES, FF, D), 1.0, 6.0, ((0, 8), (1, 32)))
    mom_up = centred(keys[10], (MODULES, D, FF), 0.5, 4.0, ((0, 8), (2, 32)), jnp.float32)
    mom_down = centred(keys[11], (MODULES, FF, D), 0.5, 4.0, ((0, 8), (1, 32)), jnp.float32)
    return dict(acts=acts, cotan=cotan, w_up=w_up, w_down=w_down, drift_up=drift_up, drift_down=drift_down, path=path, slot_of=slot_of, global_up=global_up, global_down=global_down, mom_up=mom_up, mom_down=mom_down)


def gelu_tanh(value):
    return jax.nn.gelu(value, approximate=True)

def region_grads(inputs, cotangent, weight_up, weight_down):
    hidden = jnp.dot(inputs, weight_up, preferred_element_type=jnp.float32) * D ** (-0.5)
    active, pullback = jax.vjp(gelu_tanh, hidden)
    active_b = active.astype(jnp.bfloat16)
    dactive = jnp.dot(cotangent, weight_down.T, preferred_element_type=jnp.float32) * FF ** (-0.5)
    dhidden = pullback(dactive)[0].astype(jnp.bfloat16)
    grad_down = jnp.dot(active_b.T, cotangent, preferred_element_type=jnp.float32) * FF ** (-0.5)
    grad_up = jnp.dot(inputs.T, dhidden, preferred_element_type=jnp.float32) * D ** (-0.5)
    return (grad_up, grad_down)

def reference(acts, cotan, w_up, w_down, drift_up, drift_down, path, slot_of, global_up, global_down, mom_up, mom_down):
    pseudo_up = []
    pseudo_down = []
    for region in range(N_REGION):
        grad_up, grad_down = region_grads(acts[region], cotan[region], w_up[region], w_down[region])
        pseudo_up.append((drift_up[region].astype(jnp.float32) + 0.5 * grad_up).astype(jnp.bfloat16))
        pseudo_down.append((drift_down[region].astype(jnp.float32) + 0.5 * grad_down).astype(jnp.bfloat16))
    pseudo_up = jnp.stack(pseudo_up).astype(jnp.float32)
    pseudo_down = jnp.stack(pseudo_down).astype(jnp.float32)
    target = slot_of[path].astype(jnp.int32)
    chosen = (target[:, None] == jnp.arange(MODULES, dtype=jnp.int32)[None, :]).astype(jnp.float32)
    count = lax.optimization_barrier(jnp.sum(chosen, axis=0))
    divisor = jnp.maximum(count, 1.0)[:, None, None]
    delta_up = jnp.einsum('rs,rdf->sdf', chosen, pseudo_up) / divisor
    delta_down = jnp.einsum('rs,rfd->sfd', chosen, pseudo_down) / divisor
    moment_up = 0.9 * mom_up + delta_up
    moment_down = 0.9 * mom_down + delta_down
    new_up = (global_up.astype(jnp.float32) - 0.7 * (delta_up + 0.9 * moment_up)).astype(jnp.bfloat16)
    new_down = (global_down.astype(jnp.float32) - 0.7 * (delta_down + 0.9 * moment_down)).astype(jnp.bfloat16)
    return (new_up, new_down, new_up[target], new_down[target])
```

```python
import functools
import math

import jax
import jax.numpy as jnp
from jax import lax
from jax.experimental import pallas as pl
from jax.experimental.pallas import tpu as pltpu
from jax.sharding import Mesh
from jax.sharding import PartitionSpec as P

D = 2048
FF = 4096
REGION = ("xh", "y")
DEV = ("z", "xl", "c")
NR = 8
BF = jnp.bfloat16
F32 = jnp.float32
MIB = 1 << 20


def params(mib=48):
    return pltpu.CompilerParams(vmem_limit_bytes=mib * MIB)


def whole(count):
    return [pl.BlockSpec(memory_space=pltpu.VMEM)] * count


def grads_kernel(n_blocks, first, *refs):
    blocks = refs[:n_blocks]
    up_ref, down_ref = refs[n_blocks : n_blocks + 2]
    outs = refs[-2:]
    olds = None if first else refs[n_blocks + 2 : n_blocks + 4]
    x = jnp.concatenate([b[0] for b in blocks], axis=0)
    g = jnp.concatenate([b[1] for b in blocks], axis=0)
    hid = jnp.dot(x, up_ref[...], preferred_element_type=F32) * D ** (-0.5)
    dact = lax.dot_general(
        g, down_ref[...], (((1,), (1,)), ((), ())), preferred_element_type=F32
    ) * FF ** (-0.5)
    root = math.sqrt(2.0 / math.pi)
    sq = hid * hid
    t = jnp.tanh(root * (hid + 0.044715 * (sq * hid)))
    act = (0.5 * hid * (1.0 + t)).astype(BF)
    slope = 0.5 * (1.0 + t) + 0.5 * hid * (1.0 - t * t) * (root * (1.0 + 3 * 0.044715 * sq))
    dhid = (dact * slope).astype(BF)
    gd = lax.dot_general(act, g, (((0,), (0,)), ((), ())), preferred_element_type=F32)
    gu = lax.dot_general(dhid, x, (((0,), (0,)), ((), ())), preferred_element_type=F32)
    if not first:
        gd = gd + olds[0][...]
        gu = gu + olds[1][...]
    outs[0][...] = gd
    outs[1][...] = gu


def grads_step(blocks, up2, down2, sums):
    n = len(blocks)
    first = sums is None
    tokens = sum(b.shape[1] for b in blocks)
    operands = list(blocks) + [up2, down2] + ([] if first else list(sums))
    shape = jax.ShapeDtypeStruct((256, D), F32)
    return pl.pallas_call(
        functools.partial(grads_kernel, n, first),
        out_shape=(shape, shape),
        in_specs=whole(len(operands)),
        out_specs=tuple(whole(2)),
        input_output_aliases={} if first else {n + 2: 0, n + 3: 1},
        compiler_params=params(),
        cost_estimate=pl.CostEstimate(
            flops=8 * tokens * D * 256, bytes_accessed=12 * MIB, transcendentals=tokens * 256
        ),
    )(*operands)


def part_kernel(gd_ref, gu_ref, out_ref):
    out_ref[0] = (gd_ref[128:256, :] * (0.5 * FF ** (-0.5))).astype(BF)
    out_ref[1] = (gu_ref[128:256, :] * (0.5 * D ** (-0.5))).astype(BF)


def part(sums):
    return pl.pallas_call(
        part_kernel,
        out_shape=jax.ShapeDtypeStruct((2, 128, D), BF),
        in_specs=whole(2),
        out_specs=pl.BlockSpec(memory_space=pltpu.VMEM),
        compiler_params=params(),
    )(*sums)


def down_in(eighth):
    return jnp.concatenate([eighth[:, j * 128 : (j + 1) * 128] for j in range(16)], axis=0)


def pseudo_kernel(gd_ref, gu_ref, got_ref, du_ref, dd_ref, out_ref):
    down = gd_ref[0:128, :] * (0.5 * FF ** (-0.5)) + got_ref[0].astype(F32)
    down = (down + dd_ref[0].astype(F32)).astype(BF)
    up = gu_ref[0:128, :] * (0.5 * D ** (-0.5)) + got_ref[1].astype(F32)
    for r in range(NR):
        mine = up[:, r * 256 : (r + 1) * 256].T + du_ref[0, r * 256 : (r + 1) * 256, :].astype(F32)
        out_ref[r, 0:256, :] = mine.astype(BF)
        out_ref[r, 256:512, :] = down_in(down[r * 16 : (r + 1) * 16, :])


def pseudo(sums, got, drift_up, drift_down):
    return pl.pallas_call(
        pseudo_kernel,
        out_shape=jax.ShapeDtypeStruct((NR, 512, 128), BF),
        in_specs=whole(5),
        out_specs=pl.BlockSpec(memory_space=pltpu.VMEM),
        compiler_params=params(),
    )(*sums, got, drift_up, drift_down)


def state_kernel(gu_ref, gd_ref, mu_ref, md_ref, out_ref):
    for s in range(2):
        out_ref[0, s, 0:256, :] = gu_ref[s].astype(F32) - 0.567 * mu_ref[s]
        out_ref[0, s, 256:512, :] = down_in(gd_ref[s].astype(F32) - 0.567 * md_ref[s])


def state(global_up, global_down, mom_up, mom_down):
    up = pl.BlockSpec((2, 256, 128), lambda i: (0, i, 0))
    down = pl.BlockSpec((2, 16, D), lambda i: (0, i, 0))
    return pl.pallas_call(
        state_kernel,
        grid=(NR,),
        out_shape=jax.ShapeDtypeStruct((NR, 2, 512, 128), F32),
        in_specs=[up, down, up, down],
        out_specs=pl.BlockSpec((1, 2, 512, 128), lambda i: (i, 0, 0, 0)),
        compiler_params=params(),
        cost_estimate=pl.CostEstimate(flops=4 * MIB, bytes_accessed=10 * MIB, transcendentals=0),
    )(global_up, global_down, mom_up, mom_down)


def step_kernel(target_ref, weight_ref, p_ref, a_ref, out_ref):
    for o in range(NR):
        for s in range(2):
            slot = 2 * o + s
            delta = weight_ref[0, slot] * p_ref[0].astype(F32)
            for r in range(1, NR):
                delta = delta + weight_ref[r, slot] * p_ref[r].astype(F32)
            out_ref[o, s] = (a_ref[o, s] - 1.33 * delta).astype(BF)
    for r in range(NR):
        at = target_ref[r]
        out_ref[r, 2] = out_ref[at // 2, at % 2]


def step(target, weight, pieces, base):
    rows = 128
    return pl.pallas_call(
        step_kernel,
        grid=(512 // rows,),
        out_shape=jax.ShapeDtypeStruct((NR, 3, 512, 128), BF),
        in_specs=[
            pl.BlockSpec(memory_space=pltpu.SMEM),
            pl.BlockSpec(memory_space=pltpu.SMEM),
            pl.BlockSpec((NR, rows, 128), lambda i: (0, i, 0)),
            pl.BlockSpec((NR, 2, rows, 128), lambda i: (0, 0, i, 0)),
        ],
        out_specs=pl.BlockSpec((NR, 3, rows, 128), lambda i: (0, 0, i, 0)),
        compiler_params=params(),
    )(target, weight, pieces, base)


def place_kernel(got_ref, nu_ref, nd_ref, ru_ref, rd_ref):
    def down_out(s):
        return jnp.concatenate(
            [got_ref[0, s, 256 + j * 16 : 272 + j * 16, :] for j in range(16)], axis=1
        )

    for s in range(2):
        nu_ref[s] = got_ref[0, s, 0:256, :]
        nd_ref[s] = down_out(s)
    ru_ref[0] = got_ref[0, 2, 0:256, :]
    rd_ref[0] = down_out(2)


def place(got):
    def up(n):
        return pl.BlockSpec((n, 256, 128), lambda i: (0, i, 0))

    def down(n):
        return pl.BlockSpec((n, 16, D), lambda i: (0, i, 0))

    return pl.pallas_call(
        place_kernel,
        grid=(NR,),
        out_shape=(
            jax.ShapeDtypeStruct((2, D, 128), BF),
            jax.ShapeDtypeStruct((2, 128, D), BF),
            jax.ShapeDtypeStruct((1, D, 128), BF),
            jax.ShapeDtypeStruct((1, 128, D), BF),
        ),
        in_specs=[pl.BlockSpec((1, 3, 512, 128), lambda i: (i, 0, 0, 0))],
        out_specs=(up(2), down(2), up(1), down(1)),
        compiler_params=params(),
    )(got)


RIGHT = [(i, (i + 1) % 8) for i in range(8)]
LEFT = [(i, (i + 7) % 8) for i in range(8)]
SWAP = [(0, 1), (1, 0)]


def on_device(
    acts,
    cotan,
    w_up,
    w_down,
    drift_up,
    drift_down,
    path,
    slot_of,
    global_up,
    global_down,
    mom_up,
    mom_down,
):
    module_ids = jnp.arange(slot_of.shape[0], dtype=jnp.int32)
    target = jnp.sum(jnp.where(path[:, None] == module_ids[None, :], slot_of[None, :], 0), axis=1)
    chosen = (target[:, None] == module_ids[None, :]).astype(F32)
    weight = chosen / jnp.maximum(jnp.sum(chosen, axis=0), 1.0)[None, :]

    base = state(global_up, global_down, mom_up, mom_down)
    base = lax.all_to_all(base, REGION, 0, 0, tiled=True)

    own = jnp.concatenate([acts, cotan], axis=0)
    other = lax.ppermute(own, "xl", SWAP)
    up2 = jnp.concatenate([w_up[0], lax.ppermute(w_up, "c", SWAP)[0]], axis=1)
    down2 = jnp.concatenate([w_down[0], lax.ppermute(w_down, "c", SWAP)[0]], axis=0)

    heads = [(own, own), (other, other)]
    sums = grads_step([own, other], up2, down2, None)
    for hop in range(4):
        blocks = []
        for k in range(2):
            right, left = heads[k]
            if hop == 3:
                right, left = right[:, :32], left[:, 32:]
            right = lax.ppermute(right, "z", RIGHT)
            left = lax.ppermute(left, "z", LEFT)
            heads[k] = (right, left)
            blocks += [right, left]
        sums = grads_step(blocks, up2, down2, sums)

    got = lax.ppermute(part(sums), "c", SWAP)
    pieces = pseudo(sums, got, drift_up, drift_down)
    pieces = lax.all_to_all(pieces, REGION, 0, 0, tiled=True)
    reply = step(target, weight, pieces, base)
    reply = lax.all_to_all(reply, REGION, 0, 0, tiled=True)
    return place(reply)


def solution(mesh):
    fine = Mesh(mesh.devices.reshape(2, 4, 8, 2, 2), REGION + DEV)
    rows = P(REGION, DEV, None)
    cols = P(REGION, None, DEV)
    return jax.shard_map(
        on_device,
        mesh=fine,
        in_specs=(rows, rows, cols, rows, cols, rows, P(), P(), cols, rows, cols, rows),
        out_specs=(cols, rows, cols, rows),
        check_vma=False,
    )
```

```python
import functools
import math

import jax
import jax.numpy as jnp
from jax import lax
from jax.experimental import pallas as pl
from jax.experimental.pallas import tpu as pltpu
from jax.sharding import Mesh
from jax.sharding import PartitionSpec as P

D = 2048
FF = 4096
REGION = ("xh", "y")
DEV = ("z", "xl", "c")
NR = 8
BF = jnp.bfloat16
F32 = jnp.float32
MIB = 1 << 20


def params(mib=16):
    return pltpu.CompilerParams(vmem_limit_bytes=mib * MIB)


def whole(count):
    return [pl.BlockSpec(memory_space=pltpu.VMEM)] * count


def grads_kernel(n_blocks, first, last, *refs):
    refs, (held, sems) = refs[:-2], refs[-2:]
    blocks = refs[:n_blocks]
    up_ref, down_ref = refs[n_blocks : n_blocks + 2]
    outs = refs[-2:]
    coming = []
    if not first:
        olds = refs[n_blocks + 2 : n_blocks + 4]
        coming = [pltpu.make_async_copy(olds[i], held.at[i], sems.at[i]) for i in range(2)]
    for copy in coming:
        copy.start()
    x = jnp.concatenate([b[0] for b in blocks], axis=0)
    g = jnp.concatenate([b[1] for b in blocks], axis=0)
    hid = jnp.dot(x, up_ref[...], preferred_element_type=F32) * D ** (-0.5)
    dact = lax.dot_general(
        g, down_ref[...], (((1,), (1,)), ((), ())), preferred_element_type=F32
    ) * FF ** (-0.5)
    root = math.sqrt(2.0 / math.pi)
    sq = hid * hid
    t = jnp.tanh(root * (hid + 0.044715 * (sq * hid)))
    act = (0.5 * hid * (1.0 + t)).astype(BF)
    slope = 0.5 * (1.0 + t) + 0.5 * hid * (1.0 - t * t) * (root * (1.0 + 3 * 0.044715 * sq))
    dhid = (dact * slope).astype(BF)
    for copy in coming:
        copy.wait()
    for i, (left, right, scale) in enumerate(((act, g, FF), (dhid, x, D))):
        total = lax.dot_general(left, right, (((0,), (0,)), ((), ())), preferred_element_type=F32)
        total = total * (0.5 * scale ** (-0.5))
        if not first:
            total = total + held[i]
        if last:
            outs[0][i] = total[0:128]
            outs[1][i] = total[128:256].astype(BF)
        else:
            held[i] = total
            pltpu.make_async_copy(held.at[i], outs[i], sems.at[i]).start()
    if not last:
        for i in range(2):
            pltpu.make_async_copy(held.at[i], outs[i], sems.at[i]).wait()


def grads_step(blocks, up2, down2, sums, last=False):
    n = len(blocks)
    first = sums is None
    tokens = sum(b.shape[1] for b in blocks)
    operands = list(blocks) + [up2, down2] + ([] if first else list(sums))
    shape = jax.ShapeDtypeStruct((256, D), F32)
    half = jax.ShapeDtypeStruct((2, 128, D), F32), jax.ShapeDtypeStruct((2, 128, D), BF)
    far = [pl.BlockSpec(memory_space=pltpu.HBM)] * 2
    return pl.pallas_call(
        functools.partial(grads_kernel, n, first, last),
        out_shape=half if last else (shape, shape),
        in_specs=whole(n + 2) + ([] if first else far),
        out_specs=tuple(whole(2) if last else far),
        scratch_shapes=[pltpu.VMEM((2, 256, D), F32), pltpu.SemaphoreType.DMA((2,))],
        compiler_params=params(18),
        cost_estimate=pl.CostEstimate(
            flops=20 * 10**9, bytes_accessed=64 * MIB, transcendentals=tokens * 256
        ),
    )(*operands)


def down_in(eighth):
    return jnp.concatenate([eighth[:, j * 128 : (j + 1) * 128] for j in range(16)], axis=0)


def pseudo_kernel(kept_ref, got_ref, du_ref, dd_ref, out_ref):
    down = kept_ref[0] + got_ref[0].astype(F32)
    down = (down + dd_ref[0].astype(F32)).astype(BF)
    up = kept_ref[1] + got_ref[1].astype(F32)
    for r in range(NR):
        mine = up[:, r * 256 : (r + 1) * 256].T + du_ref[0, r * 256 : (r + 1) * 256, :].astype(F32)
        out_ref[r, 0:256, :] = mine.astype(BF)
        out_ref[r, 256:512, :] = down_in(down[r * 16 : (r + 1) * 16, :])


def pseudo(kept, got, drift_up, drift_down):
    return pl.pallas_call(
        pseudo_kernel,
        out_shape=jax.ShapeDtypeStruct((NR, 512, 128), BF),
        in_specs=whole(4),
        out_specs=pl.BlockSpec(memory_space=pltpu.VMEM),
        compiler_params=params(),
    )(kept, got, drift_up, drift_down)


def state_kernel(gu_ref, gd_ref, mu_ref, md_ref, out_ref):
    for s in range(2):
        out_ref[0, s, 0:256, :] = gu_ref[s].astype(F32) - 0.567 * mu_ref[s]
        out_ref[0, s, 256:512, :] = down_in(gd_ref[s].astype(F32) - 0.567 * md_ref[s])


def state(global_up, global_down, mom_up, mom_down):
    up = pl.BlockSpec((2, 256, 128), lambda i: (0, i, 0))
    down = pl.BlockSpec((2, 16, D), lambda i: (0, i, 0))
    return pl.pallas_call(
        state_kernel,
        grid=(NR,),
        out_shape=jax.ShapeDtypeStruct((NR, 2, 512, 128), F32),
        in_specs=[up, down, up, down],
        out_specs=pl.BlockSpec((1, 2, 512, 128), lambda i: (i, 0, 0, 0)),
        compiler_params=params(),
        cost_estimate=pl.CostEstimate(flops=4 * MIB, bytes_accessed=10 * MIB, transcendentals=0),
    )(global_up, global_down, mom_up, mom_down)


def step_kernel(target_ref, factor_ref, p_ref, a_ref, out_ref, sum_ref):
    sum_ref[...] = jnp.zeros_like(sum_ref)
    for r in range(NR):
        at = target_ref[r]
        sum_ref[at] = sum_ref[at] + p_ref[r].astype(F32)
    for o in range(NR):
        for s in range(2):
            slot = 2 * o + s
            out_ref[o, s] = (a_ref[o, s] - factor_ref[slot] * sum_ref[slot]).astype(BF)
    for r in range(NR):
        at = target_ref[r]
        out_ref[r, 2] = out_ref[at // 2, at % 2]


def step(target, factor, pieces, base):
    rows = 128
    return pl.pallas_call(
        step_kernel,
        grid=(512 // rows,),
        out_shape=jax.ShapeDtypeStruct((NR, 3, 512, 128), BF),
        in_specs=[
            pl.BlockSpec(memory_space=pltpu.SMEM),
            pl.BlockSpec(memory_space=pltpu.SMEM),
            pl.BlockSpec((NR, rows, 128), lambda i: (0, i, 0)),
            pl.BlockSpec((NR, 2, rows, 128), lambda i: (0, 0, i, 0)),
        ],
        out_specs=pl.BlockSpec((NR, 3, rows, 128), lambda i: (0, 0, i, 0)),
        scratch_shapes=[pltpu.VMEM((16, rows, 128), F32)],
        compiler_params=params(16),
    )(target, factor, pieces, base)


def place_kernel(got_ref, nu_ref, nd_ref, ru_ref, rd_ref):
    for p in range(2):
        up, down = slice(p * 256, p * 256 + 256), slice(p * 16, p * 16 + 16)
        for s in range(3):
            to_up, to_down = (nu_ref, nd_ref) if s < 2 else (ru_ref, rd_ref)
            to_up[s % 2, up] = got_ref[p, s, 0:256]
            to_down[s % 2, down] = jnp.concatenate(
                [got_ref[p, s, 256 + j * 16 : 272 + j * 16, :] for j in range(16)], axis=1
            )


def place(got):
    def up(n):
        return pl.BlockSpec((n, 512, 128), lambda i: (0, i, 0))

    def down(n):
        return pl.BlockSpec((n, 32, D), lambda i: (0, i, 0))

    return pl.pallas_call(
        place_kernel,
        grid=(NR // 2,),
        out_shape=(
            jax.ShapeDtypeStruct((2, D, 128), BF),
            jax.ShapeDtypeStruct((2, 128, D), BF),
            jax.ShapeDtypeStruct((1, D, 128), BF),
            jax.ShapeDtypeStruct((1, 128, D), BF),
        ),
        in_specs=[pl.BlockSpec((2, 3, 512, 128), lambda i: (i, 0, 0, 0))],
        out_specs=(up(2), down(2), up(1), down(1)),
        compiler_params=params(16),
    )(got)


RIGHT = [(i, (i + 1) % 8) for i in range(8)]
LEFT = [(i, (i + 7) % 8) for i in range(8)]
SWAP = [(0, 1), (1, 0)]


def on_device(
    acts,
    cotan,
    w_up,
    w_down,
    drift_up,
    drift_down,
    path,
    slot_of,
    global_up,
    global_down,
    mom_up,
    mom_down,
):
    module_ids = jnp.arange(slot_of.shape[0], dtype=jnp.int32)
    target = jnp.sum(jnp.where(path[:, None] == module_ids[None, :], slot_of[None, :], 0), axis=1)
    chosen = (target[:, None] == module_ids[None, :]).astype(F32)
    factor = 1.33 / jnp.maximum(jnp.sum(chosen, axis=0), 1.0)

    own = jnp.concatenate([acts, cotan], axis=0)
    other = lax.ppermute(own, "xl", SWAP)
    up2 = jnp.concatenate([w_up[0], lax.ppermute(w_up, "c", SWAP)[0]], axis=1)
    down2 = jnp.concatenate([w_down[0], lax.ppermute(w_down, "c", SWAP)[0]], axis=0)

    base = state(global_up, global_down, mom_up, mom_down)
    heads = [(own, own), (other, other)]
    sums = grads_step([own, other], up2, down2, None)
    for hop in range(4):
        blocks = []
        for k in range(2):
            right, left = heads[k]
            if hop == 3:
                right, left = right[:, :32], left[:, 32:]
            right = lax.ppermute(right, "z", RIGHT)
            left = lax.ppermute(left, "z", LEFT)
            if k == 0 and hop == 0:
                right, left, other = lax.optimization_barrier((right, left, other))
                heads[1] = (other, other)
            if k == 1 and hop == 0:
                right, left, base = lax.optimization_barrier((right, left, base))
                base = lax.all_to_all(base, REGION, 0, 0, tiled=True)
            if k == 1 and hop == 3:
                right, base = lax.optimization_barrier((right, base))
            if k == 1 and hop < 3:
                right, left, sums = lax.optimization_barrier((right, left, sums))
            heads[k] = (right, left)
            blocks += [right, left]
        sums = grads_step(blocks, up2, down2, sums, last=hop == 3)

    kept, sent = sums
    got = lax.ppermute(sent, "c", SWAP)
    pieces = pseudo(kept, got, drift_up, drift_down)
    pieces = lax.all_to_all(pieces, REGION, 0, 0, tiled=True)
    reply = step(target, factor, pieces, base)
    reply = lax.all_to_all(reply, REGION, 0, 0, tiled=True)
    return place(reply)


def solution(mesh):
    fine = Mesh(mesh.devices.reshape(2, 4, 8, 2, 2), REGION + DEV)
    rows = P(REGION, DEV, None)
    cols = P(REGION, None, DEV)
    return jax.shard_map(
        on_device,
        mesh=fine,
        in_specs=(rows, rows, cols, rows, cols, rows, P(), P(), cols, rows, cols, rows),
        out_specs=(cols, rows, cols, rows),
        check_vma=False,
    )
```

```python
import functools
import math

import jax
import jax.numpy as jnp
from jax import lax
from jax.experimental import pallas as pl
from jax.experimental.pallas import tpu as pltpu
from jax.sharding import Mesh
from jax.sharding import PartitionSpec as P

D = 2048
FF = 4096
REGION = ("xh", "y")
DEV = ("z", "xl", "c")
NR = 8
BF = jnp.bfloat16
F32 = jnp.float32
MIB = 1 << 20


def params(mib=16):
    return pltpu.CompilerParams(vmem_limit_bytes=mib * MIB)


def whole(count):
    return [pl.BlockSpec(memory_space=pltpu.VMEM)] * count


def grads_kernel(n_blocks, *refs):
    blocks = refs[:n_blocks]
    x_ref, g_ref, up_ref, down_ref, out_ref = refs[n_blocks:]
    x = jnp.concatenate([b[0] for b in blocks] + [x_ref[0]], axis=0)
    g = jnp.concatenate([b[1] for b in blocks] + [g_ref[0]], axis=0)
    root = math.sqrt(2.0 / math.pi)
    hid = jnp.dot(x, up_ref[...], preferred_element_type=F32) * D ** (-0.5)
    dact = lax.dot_general(
        g, down_ref[...], (((1,), (1,)), ((), ())), preferred_element_type=F32
    ) * FF ** (-0.5)
    sq = hid * hid
    t = jnp.tanh(root * (hid + 0.044715 * (sq * hid)))
    act = (0.5 * hid * (1.0 + t)).astype(BF)
    slope = 0.5 * (1.0 + t) + 0.5 * hid * (1.0 - t * t) * (root * (1.0 + 3 * 0.044715 * sq))
    dhid = (dact * slope).astype(BF)
    for i, (left, right, scale) in enumerate(((act, g, FF), (dhid, x, D))):
        total = lax.dot_general(left, right, (((0,), (0,)), ((), ())), preferred_element_type=F32)
        out_ref[i] = (total * (0.5 * scale ** (-0.5))).astype(out_ref.dtype)


def grads(blocks, last_x, last_g, up2, down2, dtype):
    return pl.pallas_call(
        functools.partial(grads_kernel, len(blocks)),
        out_shape=jax.ShapeDtypeStruct((2, 256, D), dtype),
        in_specs=whole(len(blocks) + 4),
        out_specs=pl.BlockSpec(memory_space=pltpu.VMEM),
        compiler_params=params(24),
        cost_estimate=pl.CostEstimate(
            flops=8 * 512 * D * 256, bytes_accessed=8 * MIB, transcendentals=512 * 256
        ),
    )(*blocks, last_x, last_g, up2, down2)


def down_in(eighth):
    return jnp.concatenate([eighth[:, j * 128 : (j + 1) * 128] for j in range(16)], axis=0)


def pseudo_kernel(side_ref, kept_ref, got_ref, du_ref, dd_ref, out_ref):
    side = side_ref[0]
    for part in range(2):
        at = side if part == 0 else 1 - side
        cut = slice(part * 128, part * 128 + 128)
        down = kept_ref[0, cut] + got_ref[0, cut].astype(F32)
        if part == 0:
            down = down + dd_ref[0].astype(F32)
        down = down.astype(BF)
        up = kept_ref[1, cut] + got_ref[1, cut].astype(F32)
        for r in range(NR):
            mine = up[:, r * 256 : (r + 1) * 256].T
            if part == 0:
                mine = mine + du_ref[0, r * 256 : (r + 1) * 256, :].astype(F32)
            out_ref[2 * r + at, 0:256, :] = mine.astype(BF)
            out_ref[2 * r + at, 256:512, :] = down_in(down[r * 16 : (r + 1) * 16, :])


def pseudo(side, kept, got, drift_up, drift_down):
    return pl.pallas_call(
        pseudo_kernel,
        out_shape=jax.ShapeDtypeStruct((2 * NR, 512, 128), BF),
        in_specs=[pl.BlockSpec(memory_space=pltpu.SMEM)] + whole(4),
        out_specs=pl.BlockSpec(memory_space=pltpu.VMEM),
        compiler_params=params(24),
    )(side, kept, got, drift_up, drift_down)


def state_kernel(gu_ref, gd_ref, mu_ref, md_ref, out_ref):
    for s in range(2):
        out_ref[0, s, 0:256, :] = gu_ref[s].astype(F32) - 0.567 * mu_ref[s]
        out_ref[0, s, 256:512, :] = down_in(gd_ref[s].astype(F32) - 0.567 * md_ref[s])


def state(global_up, global_down, mom_up, mom_down):
    up = pl.BlockSpec((2, 256, 128), lambda i: (0, i, 0))
    down = pl.BlockSpec((2, 16, D), lambda i: (0, i, 0))
    return pl.pallas_call(
        state_kernel,
        grid=(NR,),
        out_shape=jax.ShapeDtypeStruct((NR, 2, 512, 128), F32),
        in_specs=[up, down, up, down],
        out_specs=pl.BlockSpec((1, 2, 512, 128), lambda i: (i, 0, 0, 0)),
        compiler_params=params(),
        cost_estimate=pl.CostEstimate(flops=4 * MIB, bytes_accessed=10 * MIB, transcendentals=0),
    )(global_up, global_down, mom_up, mom_down)


def step_kernel(target_ref, factor_ref, p_ref, a_ref, out_ref, sum_ref):
    sum_ref[...] = jnp.zeros_like(sum_ref)
    for r in range(NR):
        at = target_ref[r]
        both = p_ref[2 * r].astype(F32) + p_ref[2 * r + 1].astype(F32)
        sum_ref[at] = sum_ref[at] + both
    for o in range(NR):
        for s in range(2):
            slot = 2 * o + s
            out_ref[o, s] = (a_ref[o, s] - factor_ref[slot] * sum_ref[slot]).astype(BF)
    for r in range(NR):
        at = target_ref[r]
        out_ref[r, 2] = out_ref[at // 2, at % 2]


def step(target, factor, pieces, base):
    rows = 128
    return pl.pallas_call(
        step_kernel,
        grid=(512 // rows,),
        out_shape=jax.ShapeDtypeStruct((NR, 3, 512, 128), BF),
        in_specs=[
            pl.BlockSpec(memory_space=pltpu.SMEM),
            pl.BlockSpec(memory_space=pltpu.SMEM),
            pl.BlockSpec((2 * NR, rows, 128), lambda i: (0, i, 0)),
            pl.BlockSpec((NR, 2, rows, 128), lambda i: (0, 0, i, 0)),
        ],
        out_specs=pl.BlockSpec((NR, 3, rows, 128), lambda i: (0, 0, i, 0)),
        scratch_shapes=[pltpu.VMEM((16, rows, 128), F32)],
        compiler_params=params(16),
    )(target, factor, pieces, base)


def place_kernel(got_ref, nu_ref, nd_ref, ru_ref, rd_ref):
    for p in range(2):
        up, down = slice(p * 256, p * 256 + 256), slice(p * 16, p * 16 + 16)
        for s in range(3):
            to_up, to_down = (nu_ref, nd_ref) if s < 2 else (ru_ref, rd_ref)
            to_up[s % 2, up] = got_ref[p, s, 0:256]
            to_down[s % 2, down] = jnp.concatenate(
                [got_ref[p, s, 256 + j * 16 : 272 + j * 16, :] for j in range(16)], axis=1
            )


def place(got):
    def up(n):
        return pl.BlockSpec((n, 512, 128), lambda i: (0, i, 0))

    def down(n):
        return pl.BlockSpec((n, 32, D), lambda i: (0, i, 0))

    return pl.pallas_call(
        place_kernel,
        grid=(NR // 2,),
        out_shape=(
            jax.ShapeDtypeStruct((2, D, 128), BF),
            jax.ShapeDtypeStruct((2, 128, D), BF),
            jax.ShapeDtypeStruct((1, D, 128), BF),
            jax.ShapeDtypeStruct((1, 128, D), BF),
        ),
        in_specs=[pl.BlockSpec((2, 3, 512, 128), lambda i: (i, 0, 0, 0))],
        out_specs=(up(2), down(2), up(1), down(1)),
        compiler_params=params(16),
    )(got)


RIGHT = [(i, (i + 1) % 8) for i in range(8)]
LEFT = [(i, (i + 7) % 8) for i in range(8)]
SWAP = [(0, 1), (1, 0)]


def on_device(
    acts,
    cotan,
    w_up,
    w_down,
    drift_up,
    drift_down,
    path,
    slot_of,
    global_up,
    global_down,
    mom_up,
    mom_down,
):
    module_ids = jnp.arange(slot_of.shape[0], dtype=jnp.int32)
    target = jnp.sum(jnp.where(path[:, None] == module_ids[None, :], slot_of[None, :], 0), axis=1)
    chosen = (target[:, None] == module_ids[None, :]).astype(F32)
    factor = 1.33 / jnp.maximum(jnp.sum(chosen, axis=0), 1.0)

    beside = [lax.ppermute(w, "xl", SWAP) for w in (w_up, w_down)]
    across = [lax.ppermute(w, "c", SWAP) for w in (w_up, w_down)]
    base = state(global_up, global_down, mom_up, mom_down)
    own = jnp.concatenate([acts, cotan], axis=0)
    right = left = own
    blocks = [own]
    for hop in range(3):
        right, left = lax.ppermute(right, "z", RIGHT), lax.ppermute(left, "z", LEFT)
        if hop == 0:
            right, left, base = lax.optimization_barrier((right, left, base))
        here = (right, left)
        if hop == 0:
            beside[1], base = lax.optimization_barrier((beside[1], base))
            base = lax.all_to_all(base, REGION, 0, 0, tiled=True)
        if hop == 1:
            right, left, beside[0] = lax.optimization_barrier((right, left, beside[0]))
        blocks += here
    corner = [lax.ppermute(w, "c", SWAP) for w in beside]
    mine = (jnp.concatenate([w_up[0], beside[0][0]], axis=1), jnp.concatenate([w_down[0], beside[1][0]], axis=0))
    theirs = (
        jnp.concatenate([across[0][0], corner[0][0]], axis=1),
        jnp.concatenate([across[1][0], corner[1][0]], axis=0),
    )
    last_x = lax.ppermute(right[0:1], "z", RIGHT)
    last_g = lax.ppermute(left[1:2], "z", LEFT)
    sent = grads(blocks, last_x, last_g, *theirs, BF)
    got = lax.ppermute(sent, "c", SWAP)
    kept = grads(blocks, last_x, last_g, *mine, F32)

    side = lax.axis_index("xl").astype(jnp.int32)[None]
    pieces = pseudo(side, kept, got, drift_up, drift_down)
    pieces = lax.all_to_all(pieces, REGION + ("xl",), 0, 0, tiled=True)
    reply = step(target, factor, pieces, base)
    reply = lax.all_to_all(reply, REGION, 0, 0, tiled=True)
    return place(reply)


def solution(mesh):
    fine = Mesh(mesh.devices.reshape(2, 4, 8, 2, 2), REGION + DEV)
    rows = P(REGION, DEV, None)
    cols = P(REGION, None, DEV)
    return jax.shard_map(
        on_device,
        mesh=fine,
        in_specs=(rows, rows, cols, rows, cols, rows, P(), P(), cols, rows, cols, rows),
        out_specs=(cols, rows, cols, rows),
        check_vma=False,
    )
```

```python
import functools
import math

import jax
import jax.numpy as jnp
from jax import lax
from jax.experimental import pallas as pl
from jax.experimental.pallas import tpu as pltpu
from jax.sharding import Mesh
from jax.sharding import PartitionSpec as P

D = 2048
FF = 4096
REGION = ("xh", "y")
DEV = ("z", "xl", "c")
NR = 8
BF = jnp.bfloat16
F32 = jnp.float32
MIB = 1 << 20


def params(mib=16):
    return pltpu.CompilerParams(vmem_limit_bytes=mib * MIB)


def whole(count):
    return [pl.BlockSpec(memory_space=pltpu.VMEM)] * count


def grads_kernel(n_blocks, *refs):
    blocks = refs[:n_blocks]
    x_ref, g_ref, up_ref, down_ref, out_ref = refs[n_blocks:]
    x = jnp.concatenate([b[0] for b in blocks] + [x_ref[0]], axis=0)
    g = jnp.concatenate([b[1] for b in blocks] + [g_ref[0]], axis=0)
    root = math.sqrt(2.0 / math.pi)
    hid = jnp.dot(x, up_ref[...], preferred_element_type=F32) * D ** (-0.5)
    dact = lax.dot_general(
        g, down_ref[...], (((1,), (1,)), ((), ())), preferred_element_type=F32
    ) * FF ** (-0.5)
    sq = hid * hid
    t = jnp.tanh(root * (hid + 0.044715 * (sq * hid)))
    act = (0.5 * hid * (1.0 + t)).astype(BF)
    slope = 0.5 * (1.0 + t) + 0.5 * hid * (1.0 - t * t) * (root * (1.0 + 3 * 0.044715 * sq))
    dhid = (dact * slope).astype(BF)
    for i, (left, right, scale) in enumerate(((act, g, FF), (dhid, x, D))):
        total = lax.dot_general(left, right, (((0,), (0,)), ((), ())), preferred_element_type=F32)
        out_ref[i] = (total * (0.5 * scale ** (-0.5))).astype(out_ref.dtype)


def grads(blocks, last_x, last_g, up2, down2, dtype):
    return pl.pallas_call(
        functools.partial(grads_kernel, len(blocks)),
        out_shape=jax.ShapeDtypeStruct((2, 256, D), dtype),
        in_specs=whole(len(blocks) + 4),
        out_specs=pl.BlockSpec(memory_space=pltpu.VMEM),
        compiler_params=params(24),
        cost_estimate=pl.CostEstimate(
            flops=8 * 512 * D * 256, bytes_accessed=8 * MIB, transcendentals=512 * 256
        ),
    )(*blocks, last_x, last_g, up2, down2)


def down_in(eighth):
    return jnp.concatenate([eighth[:, j * 128 : (j + 1) * 128] for j in range(16)], axis=0)


def pseudo_kernel(side_ref, kept_ref, got_ref, du_ref, dd_ref, out_ref):
    side = side_ref[0]
    for part in range(2):
        at = side if part == 0 else 1 - side
        cut = slice(part * 128, part * 128 + 128)
        down = kept_ref[0, cut] + got_ref[0, cut].astype(F32)
        if part == 0:
            down = down + dd_ref[0].astype(F32)
        down = down.astype(BF)
        up = kept_ref[1, cut] + got_ref[1, cut].astype(F32)
        for r in range(NR):
            mine = up[:, r * 256 : (r + 1) * 256].T
            if part == 0:
                mine = mine + du_ref[0, r * 256 : (r + 1) * 256, :].astype(F32)
            out_ref[2 * r + at, 0:256, :] = mine.astype(BF)
            out_ref[2 * r + at, 256:512, :] = down_in(down[r * 16 : (r + 1) * 16, :])


def pseudo(side, kept, got, drift_up, drift_down):
    return pl.pallas_call(
        pseudo_kernel,
        out_shape=jax.ShapeDtypeStruct((2 * NR, 512, 128), BF),
        in_specs=[pl.BlockSpec(memory_space=pltpu.SMEM)] + whole(4),
        out_specs=pl.BlockSpec(memory_space=pltpu.VMEM),
        compiler_params=params(24),
    )(side, kept, got, drift_up, drift_down)


def state_kernel(gu_ref, gd_ref, mu_ref, md_ref, out_ref, plain_up_ref, plain_down_ref):
    for s in range(2):
        up = gu_ref[s].astype(F32) - 0.567 * mu_ref[s]
        down = gd_ref[s].astype(F32) - 0.567 * md_ref[s]
        out_ref[0, s, 0:256, :] = up
        out_ref[0, s, 256:512, :] = down_in(down)
        plain_up_ref[s] = up.astype(BF)
        plain_down_ref[s] = down.astype(BF)


def state(global_up, global_down, mom_up, mom_down):
    up = pl.BlockSpec((2, 256, 128), lambda i: (0, i, 0))
    down = pl.BlockSpec((2, 16, D), lambda i: (0, i, 0))
    operands = [
        pltpu.with_memory_space_constraint(t, pltpu.HBM)
        for t in (global_up, global_down, mom_up, mom_down)
    ]
    return pl.pallas_call(
        state_kernel,
        grid=(NR,),
        out_shape=(
            pltpu.HBM((NR, 2, 512, 128), F32),
            pltpu.HBM((2, D, 128), BF),
            pltpu.HBM((2, 128, D), BF),
        ),
        in_specs=[up, down, up, down],
        out_specs=(pl.BlockSpec((1, 2, 512, 128), lambda i: (i, 0, 0, 0)), up, down),
        compiler_params=params(),
        cost_estimate=pl.CostEstimate(flops=4 * MIB, bytes_accessed=12 * MIB, transcendentals=0),
    )(*operands)


def step_kernel(target_ref, factor_ref, p_ref, a_ref, out_ref, sum_ref):
    sum_ref[...] = jnp.zeros_like(sum_ref)
    for r in range(NR):
        at = target_ref[r]
        both = p_ref[2 * r].astype(F32) + p_ref[2 * r + 1].astype(F32)
        sum_ref[at] = sum_ref[at] + both
    for o in range(NR):
        for s in range(2):
            slot = 2 * o + s
            out_ref[o, s] = (a_ref[o, s] - factor_ref[slot] * sum_ref[slot]).astype(BF)
    for r in range(NR):
        at = target_ref[r]
        out_ref[r, 2] = out_ref[at // 2, at % 2]


def step(target, factor, pieces, base):
    rows = 128
    return pl.pallas_call(
        step_kernel,
        grid=(512 // rows,),
        out_shape=jax.ShapeDtypeStruct((NR, 3, 512, 128), BF),
        in_specs=[
            pl.BlockSpec(memory_space=pltpu.SMEM),
            pl.BlockSpec(memory_space=pltpu.SMEM),
            pl.BlockSpec((2 * NR, rows, 128), lambda i: (0, i, 0)),
            pl.BlockSpec((NR, 2, rows, 128), lambda i: (0, 0, i, 0)),
        ],
        out_specs=pl.BlockSpec((NR, 3, rows, 128), lambda i: (0, 0, i, 0)),
        scratch_shapes=[pltpu.VMEM((16, rows, 128), F32)],
        compiler_params=params(16),
    )(target, factor, pieces, base)


def short_step_kernel(target_ref, second_ref, factor_ref, p_ref, a_ref, out_ref, sum_ref):
    sum_ref[...] = jnp.zeros_like(sum_ref)
    for r in range(NR):
        at = target_ref[r]
        both = p_ref[2 * r].astype(F32) + p_ref[2 * r + 1].astype(F32)
        sum_ref[at] = sum_ref[at] + both
    for o in range(NR):
        for m, slots_ref in enumerate((second_ref, target_ref)):
            slot = slots_ref[o]
            new = a_ref[slot // 2, slot % 2] - factor_ref[slot] * sum_ref[slot]
            out_ref[o, m] = new.astype(BF)


def short_step(target, second, factor, pieces, base):
    rows = 128
    return pl.pallas_call(
        short_step_kernel,
        grid=(512 // rows,),
        out_shape=jax.ShapeDtypeStruct((NR, 2, 512, 128), BF),
        in_specs=[
            pl.BlockSpec(memory_space=pltpu.SMEM),
            pl.BlockSpec(memory_space=pltpu.SMEM),
            pl.BlockSpec(memory_space=pltpu.SMEM),
            pl.BlockSpec((2 * NR, rows, 128), lambda i: (0, i, 0)),
            pl.BlockSpec((NR, 2, rows, 128), lambda i: (0, 0, i, 0)),
        ],
        out_specs=pl.BlockSpec((NR, 2, rows, 128), lambda i: (0, 0, i, 0)),
        scratch_shapes=[pltpu.VMEM((16, rows, 128), F32)],
        compiler_params=params(16),
    )(target, second, factor, pieces, base)


def down_out(eighth):
    return jnp.concatenate([eighth[256 + j * 16 : 272 + j * 16, :] for j in range(16)], axis=1)


def short_place_kernel(plan_ref, got_ref, up_ref, down_ref, nu_ref, nd_ref, ru_ref, rd_ref):
    for s in range(2):
        source = plan_ref[s]

        @pl.when(source == 2)
        def _():
            nu_ref[s] = up_ref[0]
            nd_ref[s] = down_ref[0]

        @pl.when(source != 2)
        def _():
            for p in range(2):
                eighth = got_ref[p, jnp.minimum(source, 1)]
                nu_ref[s, p * 256 : p * 256 + 256] = eighth[0:256]
                nd_ref[s, p * 16 : p * 16 + 16] = down_out(eighth)

    for p in range(2):
        eighth = got_ref[p, 1]
        ru_ref[0, p * 256 : p * 256 + 256] = eighth[0:256]
        rd_ref[0, p * 16 : p * 16 + 16] = down_out(eighth)


def short_place(plan, got, plain_up, plain_down):
    def up(n):
        return pl.BlockSpec((n, 512, 128), lambda i, plan: (0, i, 0))

    def down(n):
        return pl.BlockSpec((n, 32, D), lambda i, plan: (0, i, 0))

    return pl.pallas_call(
        short_place_kernel,
        grid_spec=pltpu.PrefetchScalarGridSpec(
            num_scalar_prefetch=1,
            grid=(NR // 2,),
            in_specs=[
                pl.BlockSpec((2, 2, 512, 128), lambda i, plan: (i, 0, 0, 0)),
                pl.BlockSpec((1, 512, 128), lambda i, plan: (plan[2], i, 0)),
                pl.BlockSpec((1, 32, D), lambda i, plan: (plan[2], i, 0)),
            ],
            out_specs=(up(2), down(2), up(1), down(1)),
        ),
        out_shape=(
            jax.ShapeDtypeStruct((2, D, 128), BF),
            jax.ShapeDtypeStruct((2, 128, D), BF),
            jax.ShapeDtypeStruct((1, D, 128), BF),
            jax.ShapeDtypeStruct((1, 128, D), BF),
        ),
        compiler_params=params(16),
    )(plan, got, plain_up, plain_down)


def place_kernel(got_ref, nu_ref, nd_ref, ru_ref, rd_ref):
    for p in range(2):
        up, down = slice(p * 256, p * 256 + 256), slice(p * 16, p * 16 + 16)
        for s in range(3):
            to_up, to_down = (nu_ref, nd_ref) if s < 2 else (ru_ref, rd_ref)
            to_up[s % 2, up] = got_ref[p, s, 0:256]
            to_down[s % 2, down] = jnp.concatenate(
                [got_ref[p, s, 256 + j * 16 : 272 + j * 16, :] for j in range(16)], axis=1
            )


def place(got):
    def up(n):
        return pl.BlockSpec((n, 512, 128), lambda i: (0, i, 0))

    def down(n):
        return pl.BlockSpec((n, 32, D), lambda i: (0, i, 0))

    return pl.pallas_call(
        place_kernel,
        grid=(NR // 2,),
        out_shape=(
            jax.ShapeDtypeStruct((2, D, 128), BF),
            jax.ShapeDtypeStruct((2, 128, D), BF),
            jax.ShapeDtypeStruct((1, D, 128), BF),
            jax.ShapeDtypeStruct((1, 128, D), BF),
        ),
        in_specs=[pl.BlockSpec((2, 3, 512, 128), lambda i: (i, 0, 0, 0))],
        out_specs=(up(2), down(2), up(1), down(1)),
        compiler_params=params(16),
    )(got)


RIGHT = [(i, (i + 1) % 8) for i in range(8)]
LEFT = [(i, (i + 7) % 8) for i in range(8)]
SWAP = [(0, 1), (1, 0)]


def on_device(
    acts,
    cotan,
    w_up,
    w_down,
    drift_up,
    drift_down,
    path,
    slot_of,
    global_up,
    global_down,
    mom_up,
    mom_down,
):
    module_ids = jnp.arange(slot_of.shape[0], dtype=jnp.int32)
    target = jnp.sum(jnp.where(path[:, None] == module_ids[None, :], slot_of[None, :], 0), axis=1)
    chosen = (target[:, None] == module_ids[None, :]).astype(F32)
    count = jnp.sum(chosen, axis=0)
    factor = 1.33 / jnp.maximum(count, 1.0)
    taken = (count > 0.0).reshape(NR, 2)
    first = 2 * jnp.arange(NR, dtype=jnp.int32)
    owned = target // 2 == first // 2
    three = jnp.any(taken[:, 0] & taken[:, 1] & ~owned)
    second = jnp.where(owned, first + 1 - target % 2, jnp.where(taken[:, 0], first, first + 1))
    me = lax.axis_index(REGION)
    slots = 2 * me + jnp.arange(2, dtype=jnp.int32)
    source = jnp.where(slots == target[me], 1, jnp.where(slots == second[me], 0, 2))
    plan = jnp.concatenate([source, 1 - second[me][None] % 2])
    plan = plan.astype(jnp.int32)

    beside = [lax.ppermute(w, "xl", SWAP) for w in (w_up, w_down)]
    across = [lax.ppermute(w, "c", SWAP) for w in (w_up, w_down)]
    base, plain_up, plain_down = state(global_up, global_down, mom_up, mom_down)
    own = jnp.concatenate([acts, cotan], axis=0)
    right = left = own
    blocks = [own]
    for hop in range(3):
        right, left = lax.ppermute(right, "z", RIGHT), lax.ppermute(left, "z", LEFT)
        if hop == 0:
            right, left, base = lax.optimization_barrier((right, left, base))
        here = (right, left)
        if hop == 0:
            beside[1], base = lax.optimization_barrier((beside[1], base))
            base = lax.all_to_all(base, REGION, 0, 0, tiled=True)
        if hop == 1:
            right, left, beside[0] = lax.optimization_barrier((right, left, beside[0]))
        blocks += here
    corner = [lax.ppermute(w, "c", SWAP) for w in beside]
    mine = (jnp.concatenate([w_up[0], beside[0][0]], axis=1), jnp.concatenate([w_down[0], beside[1][0]], axis=0))
    theirs = (
        jnp.concatenate([across[0][0], corner[0][0]], axis=1),
        jnp.concatenate([across[1][0], corner[1][0]], axis=0),
    )
    last_x = lax.ppermute(right[0:1], "z", RIGHT)
    last_g = lax.ppermute(left[1:2], "z", LEFT)
    sent = grads(blocks, last_x, last_g, *theirs, BF)
    got = lax.ppermute(sent, "c", SWAP)
    kept = grads(blocks, last_x, last_g, *mine, F32)

    side = lax.axis_index("xl").astype(jnp.int32)[None]
    pieces = pseudo(side, kept, got, drift_up, drift_down)
    pieces = lax.all_to_all(pieces, REGION + ("xl",), 0, 0, tiled=True)
    def long_reply():
        reply = step(target, factor, pieces, base)
        return place(lax.all_to_all(reply, REGION, 0, 0, tiled=True))

    def short_reply():
        reply = short_step(target, second, factor, pieces, base)
        reply = lax.all_to_all(reply, REGION, 0, 0, tiled=True)
        return short_place(plan, reply, plain_up, plain_down)

    return tuple(lax.cond(three, long_reply, short_reply))


def solution(mesh):
    fine = Mesh(mesh.devices.reshape(2, 4, 8, 2, 2), REGION + DEV)
    rows = P(REGION, DEV, None)
    cols = P(REGION, None, DEV)
    return jax.shard_map(
        on_device,
        mesh=fine,
        in_specs=(rows, rows, cols, rows, cols, rows, P(), P(), cols, rows, cols, rows),
        out_specs=(cols, rows, cols, rows),
        check_vma=False,
    )
```
